256 devices in a mesh: blk: 64 (over x, z, core), rep: 4 (over y).
Axes of the slice: x: 4, y: 4, z: 8, core: 2. Of those that a mesh axis runs over, the one named last changes fastest.
Arguments:
- amplitudes: bfloat16 [256, 196608], P(None, ('blk', 'rep')), may hold values from -6 to 6
- panels: bfloat16 [11008, 192, 768], P(('blk', 'rep')), may hold values from -0.21875 to 0.21875
- panel_owner_index: int32 [11008, 1], P(('blk', 'rep')), may hold values from 0 to 63; in each aligned block of 43 rows (0 to 42, 43 to 85, ...) at most 2 rows name the same one
- panel_target_tile: int32 [11008], P(('blk', 'rep')), may hold values from 0 to 15
- panel_tile_mask: int32 [11008, 4], P(('blk', 'rep')), may hold values 0 or 1
- tile_sizes: int32 [1024], replicated, may hold values from 64 to 192
- tile_irreps: int32 [1024], replicated, may hold values from 0 to 1
- occ_energy: float32 [256], P('rep'), may hold values from -3 to -0.5
- vir_energy: float32 [196608], P('blk'), may hold values from 0.5 to 6
Outputs:
- doubles_update: bfloat16 [256, 196608], P('rep', 'blk')
The draws below stay inside these ranges and needn't reach their ends.
Inputs may be any that keep to these rules, and one draw needn't show every extreme that they name: `panel_owner_index`: within the 43 rows of one device no index of blk is named more than 2 times, a bound that some block reaches.
All inputs are finite; a program needn't handle non-finite values. No bound on the sum of `panel_tile_mask` on one device may be relied on, other than what follows from the above.
Results may differ from the reference program's by a relative error of at most 0.0049.
Values may be sent and summed in bfloat16 or wider, within the bound.
A program may use at most 128 MiB of HBM per device.

```python
import math
import jax
import jax.numpy as jnp
import numpy as np
from jax import lax

TILE_SLOTS = 192
AMP_TILE_COUNT = 4
DEVICE_PANELS = 43
IRREPS = 2
ROWS = 256
RESULT_TILES = 16
NT = 1024
TOTAL_PANELS = 11008
PANEL_LIMIT = 2
N_BLK = 64
DEVICES = 256


def draw_tile_sizes(key, part):
    first_key, second_key, third_key = jax.random.split(jax.random.fold_in(key, 7), 3)
    sizes_drawn = jax.random.randint(first_key, (NT,), TILE_SLOTS // 3, TILE_SLOTS + 1)
    top_place = jax.random.randint(second_key, (), 0, NT)
    low_place = (top_place + 1 + jax.random.randint(third_key, (), 0, NT - 1)) % NT
    sizes_drawn = sizes_drawn.at[top_place].set(TILE_SLOTS).at[low_place].set(TILE_SLOTS // 3)
    return sizes_drawn.astype(jnp.int32)


def touch_ends(values, own_key, least, high):
    extent = values.shape
    place = [jax.random.randint(jax.random.fold_in(own_key, axis), (), 0, extent[axis]) for axis in range(len(extent))]
    values = values.at[tuple(place)].set(least)
    longest = extent.index(max(extent))
    place[longest] = (place[longest] + 1) % extent[longest]
    return values.at[tuple(place)].set(high)


def block_scale(rng, extent, cuts, least, top_value):
    loudness, own = 1.0, jax.random.fold_in(rng, 6)
    for position, shards_of in cuts:
        draws = jnp.exp(jax.random.uniform(jax.random.fold_in(own, position), (shards_of,), jnp.float32, least / len(cuts), top_value / len(cuts)))
        loudness = loudness * jnp.repeat(draws, extent[position] // shards_of).reshape([-1 if axis == position else 1 for axis in range(len(extent))])
    return loudness


def routed_block(key, own, number, rows, amount, top, limit, slope):
    order = jax.random.permutation(key, amount)
    heavy_load, usual = portions_of(amount, rows * top, limit, slope, True), portions_of(amount, rows * top, limit, slope, False)
    places = jnp.arange(amount)

    def named(sizes, rotation):
        used = int((sizes > 0).sum())
        fixed = max(1, used // 4)
        passed = fixed + (places - fixed + rotation * (used - fixed)) % max(1, amount - fixed)
        return jnp.zeros((amount,), jnp.int32).at[order[jnp.where(places < fixed, places, passed)]].set(jnp.asarray(sizes, jnp.int32))

    sizes = jnp.where(number % 4 == 0, named(heavy_load, number // 4), named(usual, number - number // 4 - 1))
    mixed = jax.random.permutation(jax.random.fold_in(own, 3), amount)
    source_of, sink = mixed[0:amount // 2 * 2:2], mixed[1:amount // 2 * 2:2]
    margin = jnp.minimum(sizes[source_of] - 1, limit - sizes[sink]) // 2
    margin = jnp.where((source_of == order[0]) | (sink == order[0]) | (sizes[sink] == 0), 0, jnp.maximum(margin, 0))
    passed = jax.random.randint(jax.random.fold_in(own, 4), (amount // 2,), 0, 1 << 20) % (margin + 1)
    sizes = sizes.at[source_of].add(-passed).at[sink].add(passed)
    items = jnp.searchsorted(jnp.cumsum(sizes), jnp.arange(rows * top), side="right").astype(jnp.int32)
    grid = items.reshape(top, rows).T
    grid = grid[jax.random.permutation(jax.random.fold_in(own, 1), rows)]
    rotation = jax.random.randint(jax.random.fold_in(own, 2), (rows, 1), 0, top)
    return jnp.take_along_axis(grid, (jnp.arange(top)[None, :] + rotation) % top, axis=1)


def portions_of(number_of, total, bound, lean, full):
    loads = [(1 << 20) // math.isqrt(standing ** lean) + 1 for standing in range(1, number_of + 1)]
    largest = bound if full else min(bound, max(-(-total // number_of), total * loads[0] // sum(loads)))
    least = 1 if total - largest >= number_of - 1 else 0
    given, surplus = [largest] + [least] * (number_of - 1), total - largest - least * (number_of - 1)
    while surplus > 0:
        free = [i for i in range(1, number_of) if given[i] < largest] or [i for i in range(1, number_of) if given[i] < bound]
        whole, budget = sum([loads[i] for i in free]), surplus
        for i in free:
            more = min(bound - given[i], max(1, budget * loads[i] // whole), surplus)
            given[i] = given[i] + more
            surplus = surplus - more
    return np.array(given)


def gaussian(key, dims, scale, reach, cuts=(), kind=jnp.bfloat16):
    gain = block_scale(key, dims, cuts, -0.22, 0.18) if cuts else 1.0
    drawn = jax.random.normal(key, dims, jnp.float32) * scale * gain
    return jnp.minimum(jnp.maximum(drawn, -reach), reach).astype(kind)


def setup_inputs(seed: int = 0) -> dict:
    streams_of = jax.random.split(jax.random.key(seed), 10)
    amplitudes = gaussian(streams_of[0], (ROWS, NT * TILE_SLOTS), 1.0, 6.0, ((1, 256),))
    panels = gaussian(streams_of[1], (TOTAL_PANELS, TILE_SLOTS, AMP_TILE_COUNT * TILE_SLOTS), (AMP_TILE_COUNT * TILE_SLOTS) ** -0.5, 0.21875, ((0, 256),))
    panel_owner_index_keys = jax.random.split(jax.random.fold_in(streams_of[2], 1), TOTAL_PANELS // DEVICE_PANELS)
    panel_owner_index_turns = jax.random.permutation(jax.random.fold_in(streams_of[2], 3), TOTAL_PANELS // DEVICE_PANELS)
    panel_owner_index = jax.vmap(lambda own, number: routed_block(jax.random.fold_in(streams_of[2], 2), own, number, DEVICE_PANELS, N_BLK, 1, PANEL_LIMIT, 2))(panel_owner_index_keys, panel_owner_index_turns).reshape((TOTAL_PANELS, 1))
    panel_target_tile = touch_ends(jax.random.randint(streams_of[3], (TOTAL_PANELS,), 0, RESULT_TILES), jax.random.fold_in(streams_of[3], 1), 0, RESULT_TILES - 1).astype(jnp.int32)
    panel_tile_mask = touch_ends((jax.random.randint(streams_of[4], (TOTAL_PANELS, AMP_TILE_COUNT), 0, 3) < 2).astype(jnp.int32), jax.random.fold_in(streams_of[4], 1), 0, 1)
    tile_sizes = draw_tile_sizes(jax.random.fold_in(streams_of[9], 71), 0)
    tile_irreps = touch_ends(jax.random.randint(streams_of[6], (NT,), 0, IRREPS), jax.random.fold_in(streams_of[6], 1), 0, IRREPS - 1).astype(jnp.int32)
    occ_energy = jnp.clip(-3.0 + 2.5 * jax.random.uniform(streams_of[7], (ROWS,), jnp.float32) ** block_scale(streams_of[7], (ROWS,), ((0, 4),), -0.2, 0.2), -3.0, -0.5)
    vir_energy = jnp.clip(0.5 + 5.5 * jax.random.uniform(streams_of[8], (NT * TILE_SLOTS,), jnp.float32) ** block_scale(streams_of[8], (NT * TILE_SLOTS,), ((0, 64),), -0.2, 0.2), 0.5, 6.0)
    return {"amplitudes": amplitudes, "panels": panels, "panel_owner_index": panel_owner_index, "panel_target_tile": panel_target_tile, "panel_tile_mask": panel_tile_mask, "tile_sizes": tile_sizes, "tile_irreps": tile_irreps, "occ_energy": occ_energy, "vir_energy": vir_energy}


def reference(amplitudes, panels, panel_owner_index, panel_target_tile, panel_tile_mask, tile_sizes, tile_irreps, occ_energy, vir_energy):
    in_tile = jnp.arange(TILE_SLOTS, dtype=jnp.int32)
    owner_list = panel_owner_index[:, 0]

    def one_device(ladder, device):
        first_col = (device * (AMP_TILE_COUNT * TILE_SLOTS)).astype(jnp.int32)
        columns = lax.dynamic_slice_in_dim(amplitudes, first_col, AMP_TILE_COUNT * TILE_SLOTS, 1)
        sizes_here = lax.dynamic_slice_in_dim(tile_sizes, (device * AMP_TILE_COUNT).astype(jnp.int32), AMP_TILE_COUNT, 0)
        keep_cols = (in_tile[None, :] < sizes_here[:, None]).reshape(AMP_TILE_COUNT * TILE_SLOTS)
        columns = jnp.where(keep_cols[None, :], columns, jnp.zeros_like(columns))
        first_slot = (device * DEVICE_PANELS).astype(jnp.int32)
        panel_block = lax.dynamic_slice_in_dim(panels, first_slot, DEVICE_PANELS, 0)
        owners = lax.dynamic_slice_in_dim(owner_list, first_slot, DEVICE_PANELS, 0)
        targets = lax.dynamic_slice_in_dim(panel_target_tile, first_slot, DEVICE_PANELS, 0)
        masks = lax.dynamic_slice_in_dim(panel_tile_mask, first_slot, DEVICE_PANELS, 0)
        tile_target = (owners * RESULT_TILES + targets).astype(jnp.int32)
        irrep_source = lax.dynamic_slice_in_dim(tile_irreps, (device * AMP_TILE_COUNT).astype(jnp.int32), AMP_TILE_COUNT, 0)
        irrep_target = tile_irreps[tile_target]
        live_blocks = masks * (irrep_source[None, :] == irrep_target[:, None]).astype(jnp.int32)
        scaled = panel_block.astype(jnp.float32).reshape(DEVICE_PANELS, TILE_SLOTS, AMP_TILE_COUNT, TILE_SLOTS) * live_blocks.astype(jnp.float32)[:, None, :, None]
        partial_value = jnp.einsum("slk,rk->slr", scaled.reshape(DEVICE_PANELS, TILE_SLOTS, AMP_TILE_COUNT * TILE_SLOTS), columns.astype(jnp.float32), precision=lax.Precision.HIGHEST).astype(jnp.bfloat16)
        ladder = ladder.at[tile_target].add(partial_value.astype(jnp.float32))
        return ladder, None

    start = jnp.zeros((NT, TILE_SLOTS, ROWS), jnp.float32)
    ladder, unused = lax.scan(one_device, start, jnp.arange(DEVICES, dtype=jnp.int32))
    ladder_rows = ladder.reshape(NT * TILE_SLOTS, ROWS).T
    keep_out = (in_tile[None, :] < tile_sizes[:, None]).reshape(NT * TILE_SLOTS)
    denominator = occ_energy[:, None] - vir_energy[None, :]
    result = jnp.where(keep_out[None, :], ladder_rows / denominator, jnp.zeros_like(ladder_rows))
    return result.astype(jnp.bfloat16)
```

```python
import functools

import jax
import jax.numpy as jnp
from jax import lax
from jax.experimental import pallas as pl
from jax.experimental.pallas import tpu as pltpu
from jax.sharding import PartitionSpec as P

MESH = pl.DeviceIdType.MESH
NX, NZ, NC, NY = 4, 8, 2, 4
CELL = 96
CHUNKS = 3
ROWS16 = 16
LANES = 128


def place():
    b = lax.axis_index("blk")
    return b // (NZ * NC), (b // NC) % NZ, b % NC, lax.axis_index("rep")


def device(x, z, c, y):
    return (x * (NZ * NC) + z * NC + c, y)


def greet(peers):
    barrier = pltpu.get_barrier_semaphore()
    for peer in peers:
        pl.semaphore_signal(barrier, inc=1, device_id=peer, device_id_type=MESH)
    pl.semaphore_wait(barrier, len(peers))


def remote(src, dst, send, recv, peer):
    return pltpu.make_async_remote_copy(
        src_ref=src, dst_ref=dst, send_sem=send, recv_sem=recv, device_id=peer, device_id_type=MESH
    )


COLUMN = [(dy, dc) for dy in range(NY) for dc in range(NC) if (dy, dc) != (0, 0)]


def partials_kernel(
    live_ref, enc_ref, amp_ref, keep_ref, panels_hbm, out_ref, table_ref,
    panels_v, amp_v, got, mine, in_sem, s1, r1, s2, r2, s3, r3, groups,
):
    x, z, c, y = place()
    me = y * NC + c
    slots = panels_hbm.shape[0]
    reads = []
    for g, (lo, n) in enumerate(groups):
        cp = pltpu.make_async_copy(panels_hbm.at[pl.ds(lo, n)], panels_v.at[pl.ds(lo, n)], in_sem.at[g])
        cp.start()
        reads.append(cp)
    col = [device(x, z, (c + dc) % NC, (y + dy) % NY) for dy, dc in COLUMN]
    zs = [device(x, (z + d) % NZ, c, y) for d in range(1, NZ)]
    xs = [device((x + d) % NX, z, c, y) for d in range(1, NX)]
    greet(col + zs + xs)
    first = [remote(enc_ref, got.at[me], s1.at[i], r1.at[i], p) for i, p in enumerate(col)]
    for cp in first:
        cp.start()
    got[me] = enc_ref[...]
    amp_v[...] = amp_ref[...] * keep_ref[...]
    lane = lax.broadcasted_iota(jnp.int32, (1, amp_v.shape[1]), 1)
    width = panels_v.shape[1]

    def one(s, carry):
        mask = jnp.where(
            lane < 2 * width,
            jnp.where(lane < width, live_ref[s, 0], live_ref[s, 1]),
            jnp.where(lane < 3 * width, live_ref[s, 2], live_ref[s, 3]),
        ).astype(jnp.bfloat16)
        panel = panels_v[s] * mask
        acc = lax.dot_general(
            amp_v[...], panel, (((1,), (1,)), ((), ())), preferred_element_type=jnp.float32
        )
        low = acc[:, :LANES].reshape(8, 32, LANES)
        high = acc[:, LANES:].reshape(8, 32, width - LANES)
        out_ref[0, :, s] = low[:, :16].astype(jnp.bfloat16)
        out_ref[1, :, s] = low[:, 16:].astype(jnp.bfloat16)
        out_ref[2, :, s] = jnp.concatenate([high[:, :16], high[:, 16:]], axis=-1).astype(jnp.bfloat16)
        return carry

    def work(g):
        reads[g].wait()
        lo, n = groups[g]
        lax.fori_loop(lo, lo + n, one, 0)

    work(0)
    for cp in first:
        cp.wait()
    for i in range(8):
        mine[pl.ds(i, 1), :] = got[i, pl.ds(0, 1), :]
    second = [remote(mine, table_ref.at[x, z], s2.at[i], r2.at[i], p) for i, p in enumerate(zs)]
    for cp in second:
        cp.start()
    table_ref[x, z] = mine[...]
    work(1)
    for cp in second:
        cp.wait()
    third = [remote(table_ref.at[x], table_ref.at[x], s3.at[i], r3.at[i], p) for i, p in enumerate(xs)]
    for cp in third:
        cp.start()
    for g in range(2, len(groups)):
        work(g)
    for cp in third:
        cp.wait()


def partials(live, enc, amplitudes, keep, panels):
    slots, width, kdim = panels.shape
    groups = []
    lo = 0
    while lo < slots:
        n = min(9, slots - lo)
        groups.append((lo, n))
        lo += n
    vmem = pl.BlockSpec(memory_space=pltpu.VMEM)
    return pl.pallas_call(
        functools.partial(partials_kernel, groups=tuple(groups)),
        out_shape=(
            jax.ShapeDtypeStruct((CHUNKS, 8, slots, ROWS16, LANES), jnp.bfloat16),
            jax.ShapeDtypeStruct((NX, NZ, 8, LANES), jnp.int32),
        ),
        in_specs=[pl.BlockSpec(memory_space=pltpu.SMEM), vmem, vmem, vmem, pl.BlockSpec(memory_space=pl.ANY)],
        out_specs=(vmem, vmem),
        scratch_shapes=[
            pltpu.VMEM(panels.shape, jnp.bfloat16),
            pltpu.VMEM(amplitudes.shape, jnp.bfloat16),
            pltpu.VMEM((8, 8, LANES), jnp.int32),
            pltpu.VMEM((8, LANES), jnp.int32),
            pltpu.SemaphoreType.DMA((len(groups),)),
            pltpu.SemaphoreType.DMA((7,)),
            pltpu.SemaphoreType.DMA((7,)),
            pltpu.SemaphoreType.DMA((7,)),
            pltpu.SemaphoreType.DMA((7,)),
            pltpu.SemaphoreType.DMA((3,)),
            pltpu.SemaphoreType.DMA((3,)),
        ],
        compiler_params=pltpu.CompilerParams(
            collective_id=0, has_side_effects=True, vmem_limit_bytes=56 * 1024 * 1024
        ),
    )(live, enc, amplitudes, keep, panels)


def exchange_kernel(
    cell, part_hbm, slot_ref, rank_ref, out_ref,
    yr, pf, pb, smat, sown, tmat, xs_buf, xr_buf, dense, zsp, zrp, zsm, zrm, fx, fr,
    loc_sem, ys, yrs, xs, xrs, zps, zprs, zms, zmrs, cs, crs,
):
    x, z, c, y = place()
    me = y * NC + c
    slots = part_hbm.shape[2]
    total = 8 * slots
    kpad = pb.shape[1]
    col = [(((y + dy) % NY) * NC + (c + dc) % NC, device(x, z, (c + dc) % NC, (y + dy) % NY)) for dy, dc in COLUMN]
    xpeers = [device((x + d) % NX, z, c, y) for d in range(1, NX)]
    up, down = device(x, (z + 1) % NZ, c, y), device(x, (z + NZ - 1) % NZ, c, y)
    partner = device(x, z, (c + 1) % NC, y)
    greet([p for _, p in col] + xpeers + [up, down])

    def y_start(q):
        cps = [remote(part_hbm.at[q, b], yr.at[q, me], ys.at[q, i], yrs.at[q, i], p) for i, (b, p) in enumerate(col)]
        for cp in cps:
            cp.start()
        own = pltpu.make_async_copy(part_hbm.at[q, me], yr.at[q, me], loc_sem.at[q])
        own.start()
        return cps + [own]

    def merge(q):
        def widen(b, carry):
            v = yr[q, b].astype(jnp.float32)
            pf[pl.ds(b * (slots * ROWS16), slots * ROWS16), :] = v.reshape(slots * ROWS16, LANES)
            return carry

        lax.fori_loop(0, 8, widen, 0)

        def rows(i, carry):
            r = 2 * i
            a = pf[pl.ds(r, kpad, stride=ROWS16), :].astype(jnp.bfloat16)
            b = pf[pl.ds(r + 1, kpad, stride=ROWS16), :].astype(jnp.bfloat16)
            p = jnp.concatenate([a, b], axis=1)
            pb[i] = p
            m = jnp.dot(smat[...], p, preferred_element_type=jnp.float32).astype(jnp.bfloat16)
            xs_buf[q, r] = m[:, :LANES]
            xs_buf[q, r + 1] = m[:, LANES:]
            return carry

        lax.fori_loop(0, ROWS16 // 2, rows, 0)

    def x_start(q):
        cps = []
        for i, p in enumerate(xpeers):
            part = pl.ds(i * cell, cell)
            cps.append(remote(xs_buf.at[q, :, part], xr_buf.at[q, :, part], xs.at[q, i], xrs.at[q, i], p))
        for cp in cps:
            cp.start()
        return cps

    def own_part(q):
        def rows(i, carry):
            r = 2 * i
            d = jnp.dot(sown[...], pb[i], preferred_element_type=jnp.float32)
            d = d.reshape(NZ, 32, 2 * LANES)
            dense[q, :, r] = d[:, :, :LANES]
            dense[q, :, r + 1] = d[:, :, LANES:]
            return carry

        lax.fori_loop(0, ROWS16 // 2, rows, 0)

    def gather(q):
        def rows(i, carry):
            r = 2 * i
            p = jnp.concatenate([xr_buf[q, r], xr_buf[q, r + 1]], axis=1)
            d = jnp.dot(tmat[...], p, preferred_element_type=jnp.float32)
            d = d.reshape(NZ, 32, 2 * LANES)
            dense[q, :, r] += d[:, :, :LANES]
            dense[q, :, r + 1] += d[:, :, LANES:]
            return carry

        lax.fori_loop(0, ROWS16 // 2, rows, 0)

    half = ROWS16 // 2

    def z_first(q):
        far = (z + 4) % NZ
        zsp[q, 0, :half] = dense[q, far, :half].astype(jnp.bfloat16)
        zsm[q, 0, half:] = dense[q, far, half:].astype(jnp.bfloat16)
        lo, hi = pl.ds(0, half), pl.ds(half, half)
        a = remote(zsp.at[q, 0, lo], zrp.at[q, 0, lo], zps.at[q, 0], zprs.at[q, 0], up)
        b = remote(zsm.at[q, 0, hi], zrm.at[q, 0, hi], zms.at[q, 0], zmrs.at[q, 0], down)
        a.start()
        b.start()
        return a, b

    def z_step(q, t, before):
        a, b = before
        dp, dm = (z + 4 - t) % NZ, (z + 4 + t) % NZ
        a.wait()
        if t == 1:
            zsp[q, t, :half] = (dense[q, dp, :half] + zrp[q, 0, :half].astype(jnp.float32)).astype(jnp.bfloat16)
            zsp[q, t, half:] = dense[q, dp, half:].astype(jnp.bfloat16)
        else:
            zsp[q, t] = (dense[q, dp] + zrp[q, t - 1].astype(jnp.float32)).astype(jnp.bfloat16)
        a = remote(zsp.at[q, t], zrp.at[q, t], zps.at[q, t], zprs.at[q, t], up)
        a.start()
        b.wait()
        if t == 1:
            zsm[q, t, half:] = (dense[q, dm, half:] + zrm[q, 0, half:].astype(jnp.float32)).astype(jnp.bfloat16)
            zsm[q, t, :half] = dense[q, dm, :half].astype(jnp.bfloat16)
        else:
            zsm[q, t] = (dense[q, dm] + zrm[q, t - 1].astype(jnp.float32)).astype(jnp.bfloat16)
        b = remote(zsm.at[q, t], zrm.at[q, t], zms.at[q, t], zmrs.at[q, t], down)
        b.start()
        return a, b

    def z_last(q, before):
        a, b = before
        a.wait()
        b.wait()
        f = dense[q, z] + zrp[q, 3].astype(jnp.float32) + zrm[q, 3].astype(jnp.float32)
        fx[q, 0] = f[:, :16]
        fx[q, 1] = f[:, 16:]
        cp = remote(fx.at[q, 1 - c], fr.at[q], cs.at[q], crs.at[q], partner)
        cp.start()
        return cp

    def z_all(q):
        st = z_first(q)
        for t in range(1, 4):
            st = z_step(q, t, st)
        return z_last(q, st)

    ycp = y_start(0)
    iota = lax.broadcasted_iota(jnp.int32, (cell, kpad), 0)
    for i in range(3):
        smat[pl.ds(i * cell, cell), :] = (slot_ref[pl.ds(i, 1), :kpad] == iota).astype(jnp.bfloat16)
    iota = lax.broadcasted_iota(jnp.int32, (NZ * 32, kpad), 0)
    sown[...] = (slot_ref[pl.ds(3, 1), :kpad] == iota).astype(jnp.bfloat16)
    iota = lax.broadcasted_iota(jnp.int32, (NZ * 32, 3 * cell), 1)
    hit = rank_ref[:, 0:1] == iota
    for i in range(1, 3):
        hit = hit | ((rank_ref[:, i : i + 1] >= 0) & (rank_ref[:, i : i + 1] + i * cell == iota))
    tmat[...] = hit.astype(jnp.bfloat16)
    pf[pl.ds(total * ROWS16, (kpad - total) * ROWS16), :] = jnp.zeros(((kpad - total) * ROWS16, LANES), jnp.float32)

    xcp = {}
    last = {}
    for q in range(CHUNKS):
        for cp in ycp:
            cp.wait()
        if q + 1 < CHUNKS:
            ycp = y_start(q + 1)
        merge(q)
        xcp[q] = x_start(q)
        own_part(q)
        if q >= 1:
            for cp in xcp[q - 1]:
                cp.wait()
            gather(q - 1)
            last[q - 1] = z_all(q - 1)
    q = CHUNKS - 1
    for cp in xcp[q]:
        cp.wait()
    gather(q)
    last[q] = z_all(q)
    for q in range(CHUNKS):
        last[q].wait()
        out_ref[q, c] = fx[q, c]
        out_ref[q, 1 - c] = fr[q]


def exchange(cell, ident, part, slot, rank):
    slots = part.shape[2]
    kpad = (8 * slots + 15) // 16 * 16
    vmem = pl.BlockSpec(memory_space=pltpu.VMEM)
    dma = pltpu.SemaphoreType.DMA
    bf, f32 = jnp.bfloat16, jnp.float32
    zbuf = pltpu.VMEM((CHUNKS, 4, ROWS16, 32, LANES), bf)
    return pl.pallas_call(
        functools.partial(exchange_kernel, cell),
        out_shape=jax.ShapeDtypeStruct((CHUNKS, NC, ROWS16, 16, LANES), f32),
        in_specs=[pl.BlockSpec(memory_space=pl.ANY), vmem, vmem],
        out_specs=vmem,
        scratch_shapes=[
            pltpu.VMEM((CHUNKS, 8, slots, ROWS16, LANES), bf),
            pltpu.VMEM((kpad * ROWS16, LANES), f32),
            pltpu.VMEM((ROWS16 // 2, kpad, 2 * LANES), bf),
            pltpu.VMEM((3 * cell, kpad), bf),
            pltpu.VMEM((NZ * 32, kpad), bf),
            pltpu.VMEM((NZ * 32, 3 * cell), bf),
            pltpu.VMEM((CHUNKS, ROWS16, 3 * cell, LANES), bf),
            pltpu.VMEM((CHUNKS, ROWS16, 3 * cell, LANES), bf),
            pltpu.VMEM((CHUNKS, NZ, ROWS16, 32, LANES), f32),
            zbuf, zbuf, zbuf, zbuf,
            pltpu.VMEM((CHUNKS, NC, ROWS16, 16, LANES), f32),
            pltpu.VMEM((CHUNKS, ROWS16, 16, LANES), f32),
            dma((CHUNKS,)),
            dma((CHUNKS, 7)), dma((CHUNKS, 7)),
            dma((CHUNKS, 3)), dma((CHUNKS, 3)),
            dma((CHUNKS, 4)), dma((CHUNKS, 4)),
            dma((CHUNKS, 4)), dma((CHUNKS, 4)),
            dma((CHUNKS,)), dma((CHUNKS,)),
        ],
        compiler_params=pltpu.CompilerParams(
            collective_id=ident, has_side_effects=True, vmem_limit_bytes=60 * 1024 * 1024
        ),
    )(part, slot, rank)


def finish_kernel(g_ref, occ_ref, vir_ref, keep_ref, out_ref):
    def tile(t):
        blocks = []
        for c in range(NC):
            part = [g_ref[pl.ds((q * NC + c) * 256 + t, 16, stride=16), :] for q in range(CHUNKS)]
            low = jnp.concatenate(part[:2], axis=0)
            high = jnp.concatenate([part[2][:, :64], part[2][:, 64:]], axis=0)
            blocks.append(jnp.concatenate([low, high], axis=1))
        return jnp.concatenate(blocks, axis=0)

    occ = occ_ref[...]
    for t in range(8):
        pair = jnp.concatenate([tile(2 * t), tile(2 * t + 1)], axis=1)
        cols = pl.ds(t * 384, 384)
        ratio = pair / (occ - vir_ref[:, cols])
        out_ref[:, cols] = jnp.where(keep_ref[:, cols] > 0, ratio, 0.0).astype(jnp.bfloat16)


def finish(g, occ, vir, keep):
    return pl.pallas_call(
        finish_kernel,
        out_shape=jax.ShapeDtypeStruct((occ.shape[0], vir.shape[1]), jnp.bfloat16),
    )(g.reshape(CHUNKS * NC * ROWS16 * 16, LANES), occ, vir, keep)


def shards(
    amplitudes,
    panels,
    panel_owner_index,
    panel_target_tile,
    panel_tile_mask,
    tile_sizes,
    tile_irreps,
    occ_energy,
    vir_energy,
):
    x, z, c, y = place()
    blk_index = lax.axis_index("blk")
    dev = blk_index * NY + y
    slots, width, kdim = panels.shape
    tiles_here = kdim // width
    owned = 16
    in_tile = jnp.arange(width, dtype=jnp.int32)
    sizes_here = lax.dynamic_slice_in_dim(tile_sizes, dev * tiles_here, tiles_here, 0)
    keep_cols = (in_tile[None, :] < sizes_here[:, None]).reshape(1, kdim).astype(jnp.bfloat16)
    target = panel_owner_index[:, 0] * owned + panel_target_tile
    irrep_source = lax.dynamic_slice_in_dim(tile_irreps, dev * tiles_here, tiles_here, 0)
    irrep_target = tile_irreps[target]
    live = panel_tile_mask * (irrep_source[None, :] == irrep_target[:, None]).astype(jnp.int32)
    enc = jnp.where(jnp.max(live, axis=1) > 0, target, -1)
    enc = jnp.broadcast_to(jnp.pad(enc, (0, LANES - slots), constant_values=-1)[None, :], (8, LANES))
    part, table = partials(live.astype(jnp.float32), enc, amplitudes, keep_cols, panels)

    ids = table[..., :slots].reshape(NX * NZ, 8 * slots)
    group = jnp.arange(32, dtype=jnp.int32)
    hi = ((ids[..., None] >> 5) == group).astype(jnp.bfloat16)
    lo = ((ids[..., None] & 31) == group).astype(jnp.bfloat16)
    named = jnp.einsum("csh,csl->chl", hi, lo, preferred_element_type=jnp.float32) > 0
    named = named.reshape(NX, NZ, NX, NZ * 32)
    load = jnp.sum(named.astype(jnp.int32), axis=-1)
    across = jnp.arange(NX)[:, None, None] != jnp.arange(NX)[None, None, :]
    most = jnp.max(jnp.where(across, load, 0))
    plane = lax.dynamic_index_in_dim(named, z, 1, keepdims=False)
    dist = jnp.arange(1, NX)
    mine = lax.dynamic_index_in_dim(ids.reshape(NX, NZ, 8 * slots)[:, :, :], z, 1, keepdims=False)
    mine = lax.dynamic_index_in_dim(mine, x, 0, keepdims=False)
    ahead = (x + dist) % NX
    behind = (x - dist) % NX
    sends = plane[x][ahead]
    takes = plane[behind, x]
    both = jnp.concatenate([sends, takes], axis=0)
    spot = jnp.arange(NZ * 32)
    before = (spot[:, None] < spot[None, :]).astype(jnp.bfloat16)
    rank = jnp.dot(both.astype(jnp.bfloat16), before, preferred_element_type=jnp.float32).astype(jnp.int32)
    rank = jnp.where(both, rank, -1)
    rel = mine[None, :] - ahead[:, None] * (NZ * 32)
    slot = jnp.max(jnp.where(rel[:, None, :] == spot[None, :, None], rank[:3, :, None], -1), axis=1)
    own = jnp.where((mine >= x * 256) & (mine < x * 256 + 256), mine - x * 256, -1)
    slot = jnp.concatenate([slot, own[None, :]], axis=0)
    slot = jnp.pad(slot, ((0, 4), (0, 384 - 8 * slots)), constant_values=-1)
    rank_cols = jnp.pad(rank[3:].T, ((0, 0), (0, LANES - 3)), constant_values=-1)

    summed = lax.cond(
        most <= CELL,
        functools.partial(exchange, CELL, 1),
        functools.partial(exchange, NZ * 32, 2),
        part, slot, rank_cols,
    )
    sizes_owned = lax.dynamic_slice_in_dim(tile_sizes, blk_index * owned, owned, 0)
    keep_out = (in_tile[None, :] < sizes_owned[:, None]).astype(jnp.float32).reshape(1, owned * width)
    return finish(summed, occ_energy[:, None], vir_energy[None, :], keep_out)


def solution(mesh):
    return jax.shard_map(
        shards,
        mesh=mesh,
        in_specs=(
            P(None, ("blk", "rep")),
            P(("blk", "rep"), None, None),
            P(("blk", "rep"), None),
            P(("blk", "rep")),
            P(("blk", "rep"), None),
            P(),
            P(),
            P("rep"),
            P("blk"),
        ),
        out_specs=P("rep", "blk"),
        check_vma=False,
    )
```

```python
import functools

import jax
import jax.numpy as jnp
from jax import lax
from jax.experimental import pallas as pl
from jax.experimental.pallas import tpu as pltpu
from jax.sharding import PartitionSpec as P

MESH = pl.DeviceIdType.MESH
NX, NZ, NC, NY = 4, 8, 2, 4
CELL = 96
CHUNKS = 3
R = 16
LANES = 128
SEG = 48
KPAD = 8 * SEG
OWNED = 16
SPOTS = NZ * NC * OWNED
ZT = NC * OWNED
COLUMN = [(dy, dc) for dy in range(NY) for dc in range(NC) if (dy, dc) != (0, 0)]


def place():
    b = lax.axis_index("blk")
    return b // (NZ * NC), (b // NC) % NZ, b % NC, lax.axis_index("rep")


def device(x, z, c, y):
    return (x * (NZ * NC) + z * NC + c, y)


def remote(src, dst, send, recv, peer):
    return pltpu.make_async_remote_copy(
        src_ref=src, dst_ref=dst, send_sem=send, recv_sem=recv, device_id=peer, device_id_type=MESH
    )


def start(copies):
    for cp in copies:
        cp.start()
    return copies


def wait(copies):
    for cp in copies:
        cp.wait()


def ladder_kernel(
    cell, groups,
    owner_ref, target_ref, mask_ref, sizes_ref, irreps_ref, amp_ref, panels_hbm, out_ref, most_ref,
    panels_v, amp_v, part, yr, pf, pb, smat, sown, tmat, xsend, xrecv, dense,
    zsp, zrp, zsm, zrm, fx, fr, enc, got, mine, xids, cnt, zcnt, xcnt,
    in_sem, own_sem, ys, yr_sem, xs, xr_sem, zps, zpr, zms, zmr, cs, cr,
    is_, ir, jsend, jrecv, ks, kr, ls, lr,
):
    x, z, c, y = place()
    me = y * NC + c
    dev = lax.axis_index("blk") * NY + y
    slots, width, kdim = panels_v.shape
    tiles = kdim // width
    reads = start([
        pltpu.make_async_copy(panels_hbm.at[pl.ds(lo, n)], panels_v.at[pl.ds(lo, n)], in_sem.at[g])
        for g, (lo, n) in enumerate(groups)
    ])
    col = [(((y + dy) % NY) * NC + (c + dc) % NC, device(x, z, (c + dc) % NC, (y + dy) % NY)) for dy, dc in COLUMN]
    xpeers = [device((x + d) % NX, z, c, y) for d in range(1, NX)]
    zpeers = [device(x, (z + d) % NZ, c, y) for d in range(1, NZ)]
    up, down = zpeers[0], zpeers[NZ - 2]
    partner = device(x, z, (c + 1) % NC, y)
    barrier = pltpu.get_barrier_semaphore()
    peers = [p for _, p in col] + xpeers + zpeers
    for p in peers:
        pl.semaphore_signal(barrier, inc=1, device_id=p, device_id_type=MESH)

    sources = [irreps_ref[dev * tiles + j] for j in range(tiles)]

    def target_of(s):
        return owner_ref[s, 0] * OWNED + target_ref[s]

    def live_of(s):
        kind = irreps_ref[target_of(s)]
        return [jnp.where(kind == sources[j], mask_ref[s, j], 0) for j in range(tiles)]

    seg_lane = lax.broadcasted_iota(jnp.int32, (8, KPAD), 1)

    def encode(s, row):
        live = live_of(s)
        value = jnp.where(live[0] + live[1] + live[2] + live[3] > 0, target_of(s) + 1, 0)
        return jnp.where(seg_lane == me * SEG + s, value, row)

    enc[...] = lax.fori_loop(0, slots, encode, jnp.zeros((8, KPAD), jnp.int32))
    lane = lax.broadcasted_iota(jnp.int32, (1, kdim), 1)

    def by_tile(vals):
        v = vals[tiles - 1]
        for j in range(tiles - 2, -1, -1):
            v = jnp.where(lane < (j + 1) * width, vals[j], v)
        return v

    ends = by_tile([sizes_ref[dev * tiles + j] + j * width for j in range(tiles)])
    amp_v[...] = amp_ref[...] * (lane < ends).astype(jnp.bfloat16)
    pl.semaphore_wait(barrier, len(peers))
    icp = start([remote(enc, got.at[me], is_.at[i], ir.at[i], p) for i, (b, p) in enumerate(col)])
    got[me] = enc[...]

    def one(s, carry):
        mask = by_tile(live_of(s)).astype(jnp.bfloat16)
        acc = lax.dot_general(
            amp_v[...], panels_v[s] * mask, (((1,), (1,)), ((), ())), preferred_element_type=jnp.float32
        )
        low = acc[:, :LANES].reshape(8, 2 * R, LANES)
        high = acc[:, LANES:].reshape(8, 2 * R, width - LANES)
        part[0, :, s] = low[:, :R].astype(jnp.bfloat16)
        part[1, :, s] = low[:, R:].astype(jnp.bfloat16)
        part[2, :, s] = jnp.concatenate([high[:, :R], high[:, R:]], axis=-1).astype(jnp.bfloat16)
        return carry

    def y_start(q, g):
        lo, n = groups[g] if g is not None else (0, slots)
        k = g if g is not None else 0
        return start([
            remote(part.at[q, b, pl.ds(lo, n)], yr.at[q, me, pl.ds(lo, n)], ys.at[q, k, i], yr_sem.at[q, k, i], p)
            for i, (b, p) in enumerate(col)
        ])

    ycp = {0: []}
    for g, (lo, n) in enumerate(groups):
        reads[g].wait()
        lax.fori_loop(lo, lo + n, one, 0)
        ycp[0] += y_start(0, g)
    ycp[1] = y_start(1, None)
    own = start([pltpu.make_async_copy(part.at[q, me], yr.at[q, me], own_sem.at[q]) for q in range(CHUNKS)])

    wait(icp)
    row = got[0]
    for b in range(1, 8):
        row = row + got[b]
    mine[...] = row
    jcp = start([remote(mine, xids.at[i], jsend.at[i], jrecv.at[i], p) for i, p in enumerate(xpeers)])
    spot = lax.broadcasted_iota(jnp.int32, (SPOTS, KPAD), 0)
    lower = (
        lax.broadcasted_iota(jnp.int32, (SPOTS, SPOTS), 0) >= lax.broadcasted_iota(jnp.int32, (SPOTS, SPOTS), 1)
    ).astype(jnp.bfloat16)

    def ranks(ids, group):
        hit = ids - (group * SPOTS + 1) == spot
        named = jnp.max(hit.astype(jnp.float32), axis=1, keepdims=True)
        wide = jnp.broadcast_to(named, (SPOTS, LANES))
        rank = jnp.dot(lower, wide.astype(jnp.bfloat16), preferred_element_type=jnp.float32)
        return hit, rank * wide

    count = jnp.zeros((1, LANES), jnp.float32)
    for i in range(NX - 1):
        hit, rank = ranks(mine[0:1, :], (x + i + 1) % NX)
        slot = jnp.sum(jnp.where(hit, rank[:, 0:1], 0.0), axis=0, keepdims=True)
        nth = (lax.broadcasted_iota(jnp.int32, (cell, KPAD), 0) + 1).astype(jnp.float32)
        smat[pl.ds(i * cell, cell), :] = (slot == nth).astype(jnp.bfloat16)
        count = jnp.maximum(count, jnp.max(rank, axis=0, keepdims=True))
    sown[...] = (mine[0:1, :] - (x * SPOTS + 1) == spot).astype(jnp.bfloat16)
    cnt[...] = jnp.broadcast_to(count, (8, LANES))
    kcp = start([remote(cnt, zcnt.at[z], ks.at[i], kr.at[i], p) for i, p in enumerate(zpeers)])
    zcnt[z] = cnt[...]
    pf[...] = jnp.zeros(pf.shape, jnp.float32)

    def merge(q):
        def widen(b, carry):
            v = yr[q, b].astype(jnp.float32)
            pf[pl.ds(b * (SEG * R), slots * R), :] = v.reshape(slots * R, LANES)
            return carry

        lax.fori_loop(0, 8, widen, 0)

        def rows(i, carry):
            r = 2 * i
            a = pf[pl.ds(r, KPAD, stride=R), :].astype(jnp.bfloat16)
            b = pf[pl.ds(r + 1, KPAD, stride=R), :].astype(jnp.bfloat16)
            p = jnp.concatenate([a, b], axis=1)
            pb[i] = p
            m = jnp.dot(smat[...], p, preferred_element_type=jnp.float32).astype(jnp.bfloat16)
            xsend[q, r] = m[:, :LANES]
            xsend[q, r + 1] = m[:, LANES:]
            return carry

        lax.fori_loop(0, R // 2, rows, 0)

    def x_start(q):
        out = []
        for i, p in enumerate(xpeers):
            cols = pl.ds(i * cell, cell)
            out.append(remote(xsend.at[q, :, cols], xrecv.at[q, :, cols], xs.at[q, i], xr_sem.at[q, i], p))
        return start(out)

    def own_part(q):
        def rows(i, carry):
            r = 2 * i
            d = jnp.dot(sown[...], pb[i], preferred_element_type=jnp.float32).reshape(NZ, ZT, 2 * LANES)
            dense[q, :, r] = d[:, :, :LANES]
            dense[q, :, r + 1] = d[:, :, LANES:]
            return carry

        lax.fori_loop(0, R // 2, rows, 0)

    def gather(q):
        def rows(i, carry):
            r = 2 * i
            p = jnp.concatenate([xrecv[q, r], xrecv[q, r + 1]], axis=1)
            d = jnp.zeros((SPOTS, 2 * LANES), jnp.float32)
            for k in range(NX - 1):
                d += jnp.dot(tmat[k], p[k * cell : (k + 1) * cell], preferred_element_type=jnp.float32)
            d = d.reshape(NZ, ZT, 2 * LANES)
            dense[q, :, r] += d[:, :, :LANES]
            dense[q, :, r + 1] += d[:, :, LANES:]
            return carry

        lax.fori_loop(0, R // 2, rows, 0)

    half = R // 2

    def z_first(q):
        far = (z + 4) % NZ
        zsp[q, 0, :half] = dense[q, far, :half].astype(jnp.bfloat16)
        zsm[q, 0, half:] = dense[q, far, half:].astype(jnp.bfloat16)
        lo, hi = pl.ds(0, half), pl.ds(half, half)
        a = remote(zsp.at[q, 0, lo], zrp.at[q, 0, lo], zps.at[q, 0], zpr.at[q, 0], up)
        b = remote(zsm.at[q, 0, hi], zrm.at[q, 0, hi], zms.at[q, 0], zmr.at[q, 0], down)
        start([a, b])
        return a, b

    def z_step(q, t, before):
        a, b = before
        dp, dm = (z + 4 - t) % NZ, (z + 4 + t) % NZ
        a.wait()
        if t == 1:
            zsp[q, t, :half] = (dense[q, dp, :half] + zrp[q, 0, :half].astype(jnp.float32)).astype(jnp.bfloat16)
            zsp[q, t, half:] = dense[q, dp, half:].astype(jnp.bfloat16)
        else:
            zsp[q, t] = (dense[q, dp] + zrp[q, t - 1].astype(jnp.float32)).astype(jnp.bfloat16)
        a = remote(zsp.at[q, t], zrp.at[q, t], zps.at[q, t], zpr.at[q, t], up)
        a.start()
        b.wait()
        if t == 1:
            zsm[q, t, half:] = (dense[q, dm, half:] + zrm[q, 0, half:].astype(jnp.float32)).astype(jnp.bfloat16)
            zsm[q, t, :half] = dense[q, dm, :half].astype(jnp.bfloat16)
        else:
            zsm[q, t] = (dense[q, dm] + zrm[q, t - 1].astype(jnp.float32)).astype(jnp.bfloat16)
        b = remote(zsm.at[q, t], zrm.at[q, t], zms.at[q, t], zmr.at[q, t], down)
        b.start()
        return a, b

    def z_last(q, before):
        wait(before)
        f = dense[q, z] + zrp[q, 3].astype(jnp.float32) + zrm[q, 3].astype(jnp.float32)
        fx[q, 0] = f[:, :OWNED]
        fx[q, 1] = f[:, OWNED:]
        cp = remote(fx.at[q, 1 - c], fr.at[q], cs.at[q], cr.at[q], partner)
        cp.start()
        return cp

    def z_all(q):
        st = z_first(q)
        for t in range(1, 4):
            st = z_step(q, t, st)
        return z_last(q, st)

    xcp, last = {}, {}
    for q in range(CHUNKS):
        wait(ycp[q])
        own[q].wait()
        if q + 2 < CHUNKS:
            ycp[q + 2] = y_start(q + 2, None)
        merge(q)
        xcp[q] = x_start(q)
        own_part(q)
        if q == 0:
            wait(jcp)
            nth = (lax.broadcasted_iota(jnp.int32, (SPOTS, cell), 1) + 1).astype(jnp.float32)
            for i in range(NX - 1):
                _, rank = ranks(xids[i, 0:1, :], x)
                tmat[i] = (rank[:, 0:1] == nth).astype(jnp.bfloat16)
            wait(kcp)
            cnt[...] = jnp.max(zcnt[...], axis=0)
            lcp = start([remote(cnt, xcnt.at[x], ls.at[i], lr.at[i], p) for i, p in enumerate(xpeers)])
            xcnt[x] = cnt[...]
        if q >= 1:
            wait(xcp[q - 1])
            gather(q - 1)
            last[q - 1] = z_all(q - 1)
    q = CHUNKS - 1
    wait(lcp)
    most_ref[...] = jnp.max(xcnt[...], axis=0)
    wait(xcp[q])
    gather(q)
    last[q] = z_all(q)
    for q in range(CHUNKS):
        last[q].wait()
        out_ref[q, c] = fx[q, c]
        out_ref[q, 1 - c] = fr[q]


def ladder(cell, ident, owner, target, mask, sizes, irreps, amplitudes, panels):
    slots = panels.shape[0]
    groups, lo = [], 0
    while lo < slots:
        n = min(11, slots - lo)
        groups.append((lo, n))
        lo += n
    ng = len(groups)
    vmem = pl.BlockSpec(memory_space=pltpu.VMEM)
    smem = pl.BlockSpec(memory_space=pltpu.SMEM)
    dma = pltpu.SemaphoreType.DMA
    bf, f32, i32 = jnp.bfloat16, jnp.float32, jnp.int32
    zbuf = pltpu.VMEM((CHUNKS, 4, R, ZT, LANES), bf)
    return pl.pallas_call(
        functools.partial(ladder_kernel, cell, tuple(groups)),
        out_shape=(
            jax.ShapeDtypeStruct((CHUNKS, NC, R, OWNED, LANES), f32),
            jax.ShapeDtypeStruct((8, LANES), f32),
        ),
        in_specs=[smem] * 5 + [vmem, pl.BlockSpec(memory_space=pl.ANY)],
        out_specs=(vmem, vmem),
        scratch_shapes=[
            pltpu.VMEM(panels.shape, bf),
            pltpu.VMEM(amplitudes.shape, bf),
            pltpu.VMEM((CHUNKS, 8, slots, R, LANES), bf),
            pltpu.VMEM((CHUNKS, 8, slots, R, LANES), bf),
            pltpu.VMEM((KPAD * R, LANES), f32),
            pltpu.VMEM((R // 2, KPAD, 2 * LANES), bf),
            pltpu.VMEM((3 * cell, KPAD), bf),
            pltpu.VMEM((SPOTS, KPAD), bf),
            pltpu.VMEM((NX - 1, SPOTS, cell), bf),
            pltpu.VMEM((CHUNKS, R, 3 * cell, LANES), bf),
            pltpu.VMEM((CHUNKS, R, 3 * cell, LANES), bf),
            pltpu.VMEM((CHUNKS, NZ, R, ZT, LANES), f32),
            zbuf, zbuf, zbuf, zbuf,
            pltpu.VMEM((CHUNKS, NC, R, OWNED, LANES), f32),
            pltpu.VMEM((CHUNKS, R, OWNED, LANES), f32),
            pltpu.VMEM((8, KPAD), i32),
            pltpu.VMEM((8, 8, KPAD), i32),
            pltpu.VMEM((8, KPAD), i32),
            pltpu.VMEM((NX - 1, 8, KPAD), i32),
            pltpu.VMEM((8, LANES), f32),
            pltpu.VMEM((NZ, 8, LANES), f32),
            pltpu.VMEM((NX, 8, LANES), f32),
            dma((ng,)), dma((CHUNKS,)),
            dma((CHUNKS, ng, 7)), dma((CHUNKS, ng, 7)),
            dma((CHUNKS, 3)), dma((CHUNKS, 3)),
            dma((CHUNKS, 4)), dma((CHUNKS, 4)),
            dma((CHUNKS, 4)), dma((CHUNKS, 4)),
            dma((CHUNKS,)), dma((CHUNKS,)),
            dma((7,)), dma((7,)),
            dma((3,)), dma((3,)),
            dma((7,)), dma((7,)),
            dma((3,)), dma((3,)),
        ],
        compiler_params=pltpu.CompilerParams(
            collective_id=ident, has_side_effects=True, vmem_limit_bytes=62 * 1024 * 1024
        ),
    )(owner, target, mask, sizes, irreps, amplitudes, panels)


def finish_kernel(sizes_ref, g_ref, occ_ref, vir_ref, out_ref):
    rows, cols_all = out_ref.shape
    first = lax.axis_index("blk") * OWNED
    wide = 2 * cols_all // OWNED
    lane = lax.broadcasted_iota(jnp.int32, (1, wide), 1)
    square = lax.broadcasted_iota(jnp.int32, (rows, rows), 0) == lax.broadcasted_iota(jnp.int32, (rows, rows), 1)
    occ = jnp.sum(jnp.where(square, occ_ref[...], 0.0), axis=1, keepdims=True)

    def tile(t):
        blocks = []
        for c in range(NC):
            piece = [g_ref[pl.ds((q * NC + c) * R * OWNED + t, R, stride=OWNED), :] for q in range(CHUNKS)]
            low = jnp.concatenate(piece[:2], axis=0)
            high = jnp.concatenate([piece[2][:, : LANES // 2], piece[2][:, LANES // 2 :]], axis=0)
            blocks.append(jnp.concatenate([low, high], axis=1))
        return jnp.concatenate(blocks, axis=0)

    for t in range(0, OWNED, 2):
        pair = jnp.concatenate([tile(t), tile(t + 1)], axis=1)
        cols = pl.ds(t * wide // 2, wide)
        ends = jnp.where(lane < wide // 2, sizes_ref[first + t], sizes_ref[first + t + 1] + wide // 2)
        ratio = pair / (occ - vir_ref[:, cols])
        out_ref[:, cols] = jnp.where(lane < ends, ratio, 0.0).astype(jnp.bfloat16)


def finish(sizes, g, occ, vir):
    vmem = pl.BlockSpec(memory_space=pltpu.VMEM)
    return pl.pallas_call(
        finish_kernel,
        out_shape=jax.ShapeDtypeStruct((occ.shape[1], vir.shape[1]), jnp.bfloat16),
        in_specs=[pl.BlockSpec(memory_space=pltpu.SMEM), vmem, vmem, vmem],
        out_specs=vmem,
    )(sizes, g.reshape(CHUNKS * NC * R * OWNED, LANES), occ, vir)


def shards(
    amplitudes,
    panels,
    panel_owner_index,
    panel_target_tile,
    panel_tile_mask,
    tile_sizes,
    tile_irreps,
    occ_energy,
    vir_energy,
):
    args = (panel_owner_index, panel_target_tile, panel_tile_mask, tile_sizes, tile_irreps, amplitudes, panels)
    summed, most = ladder(CELL, 0, *args)
    summed = lax.cond(
        most[0, 0] <= CELL,
        lambda first, *rest: first,
        lambda first, *rest: ladder(SPOTS, 1, *rest)[0],
        summed, *args,
    )
    return finish(tile_sizes, summed, occ_energy[None, :], vir_energy[None, :])


def solution(mesh):
    return jax.shard_map(
        shards,
        mesh=mesh,
        in_specs=(
            P(None, ("blk", "rep")),
            P(("blk", "rep"), None, None),
            P(("blk", "rep"), None),
            P(("blk", "rep")),
            P(("blk", "rep"), None),
            P(),
            P(),
            P("rep"),
            P("blk"),
        ),
        out_specs=P("rep", "blk"),
        check_vma=False,
    )
```

```python
import functools

import jax
import jax.numpy as jnp
from jax import lax
from jax.experimental import pallas as pl
from jax.experimental.pallas import tpu as pltpu
from jax.sharding import PartitionSpec as P

MESH = pl.DeviceIdType.MESH
NX, NZ, NC, NY = 4, 8, 2, 4
CELL = 96
CHUNKS = 3
R = 16
LANES = 128
SEG = 48
KPAD = 8 * SEG
OWNED = 16
SPOTS = NZ * NC * OWNED
ZT = NC * OWNED
HALF = R // 2
PLAN = [
    ("x", 0), ("y", 1), ("z", 0, 1), ("x", 1), ("z", 0, 2), ("z", 1, 1), ("z", 0, 3), ("z", 1, 2), ("x", 2),
    ("z", 0, 4), ("z", 1, 3), ("y", 2), ("z", 2, 1), ("x", 3), ("z", 1, 4), ("z", 2, 2), ("z", 3, 1), ("z", 2, 3),
    ("z", 3, 2), ("x", 4), ("z", 2, 4), ("z", 3, 3), ("z", 4, 1), ("z", 4, 2), ("z", 3, 4), ("z", 4, 3), ("x", 5),
    ("z", 5, 1), ("z", 4, 4), ("z", 5, 2), ("z", 5, 3), ("z", 5, 4),
]
COLUMN = [(dy, dc) for dy in range(NY) for dc in range(NC) if (dy, dc) != (0, 0)]


def place():
    b = lax.axis_index("blk")
    return b // (NZ * NC), (b // NC) % NZ, b % NC, lax.axis_index("rep")


def device(x, z, c, y):
    return (x * (NZ * NC) + z * NC + c, y)


def remote(src, dst, send, recv, peer):
    return pltpu.make_async_remote_copy(
        src_ref=src, dst_ref=dst, send_sem=send, recv_sem=recv, device_id=peer, device_id_type=MESH
    )


def start(copies):
    for cp in copies:
        cp.start()
    return copies


def wait(copies):
    for cp in copies:
        cp.wait()


def ladder_kernel(
    cell, groups,
    owner_ref, target_ref, mask_ref, sizes_ref, irreps_ref, amp_ref, panels_hbm, out_ref, most_ref,
    panels_v, amp_v, part, yr, pf, pb, smat, sown, tmat, xsend, xrecv, dense,
    zsp, zrp, zsm, zrm, fx, fr, enc, got, mine, xids, cnt, zcnt, xcnt,
    in_sem, own_sem, ys, yr_sem, xs, xr_sem, zps, zpr, zms, zmr, cs, cr,
    is_, ir, jsend, jrecv, ks, kr, ls, lr,
):
    x, z, c, y = place()
    me = y * NC + c
    dev = lax.axis_index("blk") * NY + y
    slots, width, kdim = panels_v.shape
    tiles = kdim // width
    reads = start([
        pltpu.make_async_copy(panels_hbm.at[pl.ds(lo, n)], panels_v.at[pl.ds(lo, n)], in_sem.at[g])
        for g, (lo, n) in enumerate(groups)
    ])
    col = [(((y + dy) % NY) * NC + (c + dc) % NC, device(x, z, (c + dc) % NC, (y + dy) % NY)) for dy, dc in COLUMN]
    xpeers = [device((x + d) % NX, z, c, y) for d in range(1, NX)]
    zpeers = [device(x, (z + d) % NZ, c, y) for d in range(1, NZ)]
    up, down = zpeers[0], zpeers[NZ - 2]
    partner = device(x, z, (c + 1) % NC, y)
    barrier = pltpu.get_barrier_semaphore()
    peers = [p for _, p in col] + xpeers + zpeers
    for p in peers:
        pl.semaphore_signal(barrier, inc=1, device_id=p, device_id_type=MESH)

    sources = [irreps_ref[dev * tiles + j] for j in range(tiles)]

    def target_of(s):
        return owner_ref[s] * OWNED + target_ref[s]

    def live_of(s):
        kind = irreps_ref[target_of(s)]
        return [jnp.where(kind == sources[j], mask_ref[j, s], 0) for j in range(tiles)]

    seg_lane = lax.broadcasted_iota(jnp.int32, (8, KPAD), 1)

    def encode(s, row):
        live = live_of(s)
        value = jnp.where(live[0] + live[1] + live[2] + live[3] > 0, target_of(s) + 1, 0)
        return jnp.where(seg_lane == me * SEG + s, value, row)

    lane = lax.broadcasted_iota(jnp.int32, (1, kdim), 1)

    def by_tile(vals):
        v = vals[tiles - 1]
        for j in range(tiles - 2, -1, -1):
            v = jnp.where(lane < (j + 1) * width, vals[j], v)
        return v

    ends = by_tile([sizes_ref[dev * tiles + j] + j * width for j in range(tiles)])
    amp_v[...] = amp_ref[...] * (lane < ends).astype(jnp.bfloat16)

    def one(s, carry):
        mask = by_tile(live_of(s)).astype(jnp.bfloat16)
        acc = lax.dot_general(
            amp_v[...], panels_v[s] * mask, (((1,), (1,)), ((), ())), preferred_element_type=jnp.float32
        )
        low = acc[:, :LANES].reshape(8, 2 * R, LANES)
        high = acc[:, LANES:].reshape(8, 2 * R, width - LANES)
        part[0, :, s] = low[:, :R].astype(jnp.bfloat16)
        part[1, :, s] = low[:, R:].astype(jnp.bfloat16)
        part[2, :, s] = jnp.concatenate([high[:, :R], high[:, R:]], axis=-1).astype(jnp.bfloat16)
        return carry

    def y_start(q, g):
        lo, n = groups[g] if g is not None else (0, slots)
        k = g if g is not None else 0
        return start([
            remote(part.at[q, b, pl.ds(lo, n)], yr.at[q, me, pl.ds(lo, n)], ys.at[q, k, i], yr_sem.at[q, k, i], p)
            for i, (b, p) in enumerate(col)
        ])

    ycp = {0: []}
    for g, (lo, n) in enumerate(groups):
        reads[g].wait()
        lax.fori_loop(lo, lo + n, one, 0)
        if g == 0:
            pl.semaphore_wait(barrier, len(peers))
        ycp[0] += y_start(0, g)
        if g == 1:
            enc[...] = lax.fori_loop(0, slots, encode, jnp.zeros((8, KPAD), jnp.int32))
            icp = start([remote(enc, got.at[me], is_.at[i], ir.at[i], p) for i, (b, p) in enumerate(col)])
            got[me] = enc[...]
    ycp[1] = y_start(1, None)
    own = start([pltpu.make_async_copy(part.at[q, me], yr.at[q, me], own_sem.at[q]) for q in range(CHUNKS)])

    wait(icp)
    row = got[0]
    for b in range(1, 8):
        row = row + got[b]
    mine[...] = row
    jcp = start([remote(mine, xids.at[i], jsend.at[i], jrecv.at[i], p) for i, p in enumerate(xpeers)])
    spot = lax.broadcasted_iota(jnp.int32, (SPOTS, KPAD), 0)
    lower = (
        lax.broadcasted_iota(jnp.int32, (SPOTS, SPOTS), 0) >= lax.broadcasted_iota(jnp.int32, (SPOTS, SPOTS), 1)
    ).astype(jnp.bfloat16)

    def ranks(ids, group):
        hit = ids - (group * SPOTS + 1) == spot
        named = jnp.max(hit.astype(jnp.float32), axis=1, keepdims=True)
        wide = jnp.broadcast_to(named, (SPOTS, LANES))
        rank = jnp.dot(lower, wide.astype(jnp.bfloat16), preferred_element_type=jnp.float32)
        return hit, rank * wide

    count = jnp.zeros((1, LANES), jnp.float32)
    for i in range(NX - 1):
        hit, rank = ranks(mine[0:1, :], (x + i + 1) % NX)
        slot = jnp.sum(jnp.where(hit, rank[:, 0:1], 0.0), axis=0, keepdims=True)
        nth = (lax.broadcasted_iota(jnp.int32, (cell, KPAD), 0) + 1).astype(jnp.float32)
        smat[pl.ds(i * cell, cell), :] = (slot == nth).astype(jnp.bfloat16)
        count = jnp.maximum(count, jnp.max(rank, axis=0, keepdims=True))
    sown[...] = (mine[0:1, :] - (x * SPOTS + 1) == spot).astype(jnp.bfloat16)
    cnt[...] = jnp.broadcast_to(count, (8, LANES))
    kcp = start([remote(cnt, zcnt.at[z], ks.at[i], kr.at[i], p) for i, p in enumerate(zpeers)])
    zcnt[z] = cnt[...]
    pf[...] = jnp.zeros(pf.shape, jnp.float32)

    def merge(q):
        def widen(b, carry):
            v = yr[q, b].astype(jnp.float32)
            pf[pl.ds(b * (SEG * R), slots * R), :] = v.reshape(slots * R, LANES)
            return carry

        lax.fori_loop(0, 8, widen, 0)

    def x_start(q, h):
        def rows(i, carry):
            r = 2 * i
            a = pf[pl.ds(r, KPAD, stride=R), :].astype(jnp.bfloat16)
            b = pf[pl.ds(r + 1, KPAD, stride=R), :].astype(jnp.bfloat16)
            p = jnp.concatenate([a, b], axis=1)
            pb[i] = p
            m = jnp.dot(smat[...], p, preferred_element_type=jnp.float32).astype(jnp.bfloat16)
            xsend[q, r] = m[:, :LANES]
            xsend[q, r + 1] = m[:, LANES:]
            return carry

        lax.fori_loop(h * HALF // 2, (h + 1) * HALF // 2, rows, 0)
        out = []
        for i, p in enumerate(xpeers):
            at = (q, pl.ds(h * HALF, HALF), pl.ds(i * cell, cell))
            out.append(remote(xsend.at[at], xrecv.at[at], xs.at[q, h, i], xr_sem.at[q, h, i], p))
        return start(out)

    def own_part(q):
        def rows(i, carry):
            r = 2 * i
            d = jnp.dot(sown[...], pb[i], preferred_element_type=jnp.float32).reshape(NZ, ZT, 2 * LANES)
            dense[q, :, r] = d[:, :, :LANES]
            dense[q, :, r + 1] = d[:, :, LANES:]
            return carry

        lax.fori_loop(0, R // 2, rows, 0)

    def gather(q, h):
        def rows(i, carry):
            r = 2 * i
            p = jnp.concatenate([xrecv[q, r], xrecv[q, r + 1]], axis=1)
            d = jnp.zeros((SPOTS, 2 * LANES), jnp.float32)
            for k in range(NX - 1):
                d += jnp.dot(tmat[k], p[k * cell : (k + 1) * cell], preferred_element_type=jnp.float32)
            d = d.reshape(NZ, ZT, 2 * LANES)
            dense[q, :, r] += d[:, :, :LANES]
            dense[q, :, r + 1] += d[:, :, LANES:]
            return carry

        lax.fori_loop(h * HALF // 2, (h + 1) * HALF // 2, rows, 0)

    def z_step(q, h, t):
        lo, mid, hi = h * HALF, h * HALF + HALF // 2, (h + 1) * HALF
        all_rows, first, second = slice(lo, hi), slice(lo, mid), slice(mid, hi)
        ways = (
            (zsp, zrp, zps, zpr, up, (z + 4 - t) % NZ, first, second),
            (zsm, zrm, zms, zmr, down, (z + 4 + t) % NZ, second, first),
        )
        out = []
        for w, (zs, zr, ss, rs, peer, d, near, rest) in enumerate(ways):
            if t > 0:
                zcp[q, h][w].wait()
            if t == 0:
                zs[q, 0, near] = dense[q, d, near].astype(jnp.bfloat16)
                at = (q, 0, pl.ds(near.start, HALF // 2))
            else:
                at = (q, t, pl.ds(lo, HALF))
                if t == 1:
                    zs[q, 1, near] = (dense[q, d, near] + zr[q, 0, near].astype(jnp.float32)).astype(jnp.bfloat16)
                    zs[q, 1, rest] = dense[q, d, rest].astype(jnp.bfloat16)
                else:
                    both = dense[q, d, all_rows] + zr[q, t - 1, all_rows].astype(jnp.float32)
                    zs[q, t, all_rows] = both.astype(jnp.bfloat16)
            out.append(remote(zs.at[at], zr.at[at], ss.at[q, h, t], rs.at[q, h, t], peer))
            out[-1].start()
        zcp[q, h] = out

    def z_last(q, h):
        wait(zcp[q, h])
        at = slice(h * HALF, (h + 1) * HALF)
        f = dense[q, z, at] + zrp[q, 3, at].astype(jnp.float32) + zrm[q, 3, at].astype(jnp.float32)
        fx[q, 0, at] = f[:, :OWNED]
        fx[q, 1, at] = f[:, OWNED:]
        span = pl.ds(h * HALF, HALF)
        last[q, h] = remote(fx.at[q, 1 - c, span], fr.at[q, span], cs.at[q, h], cr.at[q, h], partner)
        last[q, h].start()

    xcp, zcp, last = {}, {}, {}

    def take_y(q):
        wait(ycp[q])
        own[q].wait()
        if q + 2 < CHUNKS:
            ycp[q + 2] = y_start(q + 2, None)
        merge(q)
        for h in range(2):
            xcp[q, h] = x_start(q, h)
        own_part(q)

    def take_x(q, h):
        wait(xcp[q, h])
        gather(q, h)
        z_step(q, h, 0)

    def zstep(u, t):
        q, h = u // 2, u % 2
        if t < 4:
            z_step(q, h, t)
        else:
            z_last(q, h)

    take_y(0)
    wait(jcp)
    nth = (lax.broadcasted_iota(jnp.int32, (SPOTS, cell), 1) + 1).astype(jnp.float32)
    for i in range(NX - 1):
        _, rank = ranks(xids[i, 0:1, :], x)
        tmat[i] = (rank[:, 0:1] == nth).astype(jnp.bfloat16)
    wait(kcp)
    cnt[...] = jnp.max(zcnt[...], axis=0)
    lcp = start([remote(cnt, xcnt.at[x], ls.at[i], lr.at[i], p) for i, p in enumerate(xpeers)])
    xcnt[x] = cnt[...]
    for step in PLAN:
        if step[0] == "y":
            take_y(step[1])
        elif step[0] == "x":
            take_x(step[1] // 2, step[1] % 2)
        else:
            zstep(step[1], step[2])
    wait(lcp)
    most_ref[...] = jnp.max(xcnt[...], axis=0)
    for q in range(CHUNKS):
        for h in range(2):
            last[q, h].wait()
        out_ref[q, c] = fx[q, c]
        out_ref[q, 1 - c] = fr[q]


def ladder(cell, ident, owner, target, mask, sizes, irreps, amplitudes, panels):
    slots = panels.shape[0]
    groups, lo = [], 0
    while lo < slots:
        n = min(13 if groups else 5, slots - lo)
        groups.append((lo, n))
        lo += n
    ng = len(groups)
    vmem = pl.BlockSpec(memory_space=pltpu.VMEM)
    smem = pl.BlockSpec(memory_space=pltpu.SMEM)
    dma = pltpu.SemaphoreType.DMA
    bf, f32, i32 = jnp.bfloat16, jnp.float32, jnp.int32
    zbuf = pltpu.VMEM((CHUNKS, 4, R, ZT, LANES), bf)
    return pl.pallas_call(
        functools.partial(ladder_kernel, cell, tuple(groups)),
        out_shape=(
            jax.ShapeDtypeStruct((CHUNKS, NC, R, OWNED, LANES), f32),
            jax.ShapeDtypeStruct((8, LANES), f32),
        ),
        in_specs=[smem] * 5 + [vmem, pl.BlockSpec(memory_space=pl.ANY)],
        out_specs=(vmem, vmem),
        scratch_shapes=[
            pltpu.VMEM(panels.shape, bf),
            pltpu.VMEM(amplitudes.shape, bf),
            pltpu.VMEM((CHUNKS, 8, slots, R, LANES), bf),
            pltpu.VMEM((CHUNKS, 8, slots, R, LANES), bf),
            pltpu.VMEM((KPAD * R, LANES), f32),
            pltpu.VMEM((R // 2, KPAD, 2 * LANES), bf),
            pltpu.VMEM((3 * cell, KPAD), bf),
            pltpu.VMEM((SPOTS, KPAD), bf),
            pltpu.VMEM((NX - 1, SPOTS, cell), bf),
            pltpu.VMEM((CHUNKS, R, 3 * cell, LANES), bf),
            pltpu.VMEM((CHUNKS, R, 3 * cell, LANES), bf),
            pltpu.VMEM((CHUNKS, NZ, R, ZT, LANES), f32),
            zbuf, zbuf, zbuf, zbuf,
            pltpu.VMEM((CHUNKS, NC, R, OWNED, LANES), f32),
            pltpu.VMEM((CHUNKS, R, OWNED, LANES), f32),
            pltpu.VMEM((8, KPAD), i32),
            pltpu.VMEM((8, 8, KPAD), i32),
            pltpu.VMEM((8, KPAD), i32),
            pltpu.VMEM((NX - 1, 8, KPAD), i32),
            pltpu.VMEM((8, LANES), f32),
            pltpu.VMEM((NZ, 8, LANES), f32),
            pltpu.VMEM((NX, 8, LANES), f32),
            dma((ng,)), dma((CHUNKS,)),
            dma((CHUNKS, ng, 7)), dma((CHUNKS, ng, 7)),
            dma((CHUNKS, 2, 3)), dma((CHUNKS, 2, 3)),
            dma((CHUNKS, 2, 4)), dma((CHUNKS, 2, 4)),
            dma((CHUNKS, 2, 4)), dma((CHUNKS, 2, 4)),
            dma((CHUNKS, 2)), dma((CHUNKS, 2)),
            dma((7,)), dma((7,)),
            dma((3,)), dma((3,)),
            dma((7,)), dma((7,)),
            dma((3,)), dma((3,)),
        ],
        compiler_params=pltpu.CompilerParams(
            collective_id=ident, has_side_effects=True, vmem_limit_bytes=62 * 1024 * 1024
        ),
    )(owner, target, mask, sizes, irreps, amplitudes, panels)


def finish_kernel(sizes_ref, g_ref, occ_ref, vir_ref, out_ref):
    rows, cols_all = out_ref.shape
    first = lax.axis_index("blk") * OWNED
    wide = 2 * cols_all // OWNED
    lane = lax.broadcasted_iota(jnp.int32, (1, wide), 1)
    square = lax.broadcasted_iota(jnp.int32, (rows, rows), 0) == lax.broadcasted_iota(jnp.int32, (rows, rows), 1)
    occ = jnp.sum(jnp.where(square, occ_ref[...], 0.0), axis=1, keepdims=True)

    def tile(t):
        blocks = []
        for c in range(NC):
            piece = [g_ref[pl.ds((q * NC + c) * R * OWNED + t, R, stride=OWNED), :] for q in range(CHUNKS)]
            low = jnp.concatenate(piece[:2], axis=0)
            high = jnp.concatenate([piece[2][:, : LANES // 2], piece[2][:, LANES // 2 :]], axis=0)
            blocks.append(jnp.concatenate([low, high], axis=1))
        return jnp.concatenate(blocks, axis=0)

    for t in range(0, OWNED, 2):
        pair = jnp.concatenate([tile(t), tile(t + 1)], axis=1)
        cols = pl.ds(t * wide // 2, wide)
        ends = jnp.where(lane < wide // 2, sizes_ref[first + t], sizes_ref[first + t + 1] + wide // 2)
        ratio = pair / (occ - vir_ref[:, cols])
        out_ref[:, cols] = jnp.where(lane < ends, ratio, 0.0).astype(jnp.bfloat16)


def finish(sizes, g, occ, vir):
    vmem = pl.BlockSpec(memory_space=pltpu.VMEM)
    return pl.pallas_call(
        finish_kernel,
        out_shape=jax.ShapeDtypeStruct((occ.shape[1], vir.shape[1]), jnp.bfloat16),
        in_specs=[pl.BlockSpec(memory_space=pltpu.SMEM), vmem, vmem, vmem],
        out_specs=vmem,
    )(sizes, g.reshape(CHUNKS * NC * R * OWNED, LANES), occ, vir)


def shards(
    amplitudes,
    panels,
    panel_owner_index,
    panel_target_tile,
    panel_tile_mask,
    tile_sizes,
    tile_irreps,
    occ_energy,
    vir_energy,
):
    args = (panel_owner_index[:, 0], panel_target_tile, panel_tile_mask.T, tile_sizes, tile_irreps, amplitudes, panels)
    summed, most = ladder(CELL, 0, *args)
    summed = lax.cond(
        most[0, 0] <= CELL,
        lambda first, *rest: first,
        lambda first, *rest: ladder(SPOTS, 1, *rest)[0],
        summed, *args,
    )
    return finish(tile_sizes, summed, occ_energy[None, :], vir_energy[None, :])


def solution(mesh):
    return jax.shard_map(
        shards,
        mesh=mesh,
        in_specs=(
            P(None, ("blk", "rep")),
            P(("blk", "rep"), None, None),
            P(("blk", "rep"), None),
            P(("blk", "rep")),
            P(("blk", "rep"), None),
            P(),
            P(),
            P("rep"),
            P("blk"),
        ),
        out_specs=P("rep", "blk"),
        check_vma=False,
    )
```

```python
import functools

import jax
import jax.numpy as jnp
from jax import lax
from jax.experimental import pallas as pl
from jax.experimental.pallas import tpu as pltpu
from jax.sharding import PartitionSpec as P

MESH = pl.DeviceIdType.MESH
NX, NZ, NC, NY = 4, 8, 2, 4
CELL = 96
CHUNKS = 3
R = 16
LANES = 128
SEG = 48
KPAD = 8 * SEG
OWNED = 16
SPOTS = NZ * NC * OWNED
ZT = NC * OWNED
UNITS = ((0, 0, 16), (1, 0, 16), (2, 0, 8), (2, 8, 8))
NU = len(UNITS)
PLAN = (
    ['s', 'y1', 'm1', 'x0', 'z01', 'z02', 'y2', 'm2', 'm3', 'z03', 'z04', 'x1', 'z11', 'z12', 'z13']
    + ['x2', 'x3', 'z14', 'z21', 'z31', 'z22', 'z32', 'z23', 'z33', 'z24', 'z34']
)
COLUMN = [(dy, dc) for dy in range(NY) for dc in range(NC) if (dy, dc) != (0, 0)]


def place():
    b = lax.axis_index("blk")
    return b // (NZ * NC), (b // NC) % NZ, b % NC, lax.axis_index("rep")


def device(x, z, c, y):
    return (x * (NZ * NC) + z * NC + c, y)


def remote(src, dst, send, recv, peer):
    return pltpu.make_async_remote_copy(
        src_ref=src, dst_ref=dst, send_sem=send, recv_sem=recv, device_id=peer, device_id_type=MESH
    )


def start(copies):
    for cp in copies:
        cp.start()
    return copies


def wait(copies):
    for cp in copies:
        cp.wait()


def ladder_kernel(
    cell, groups,
    owner_in, target_in, mask_in, sizes_in, irreps_in, amp_in, panels_hbm, out_ref, most_ref,
    owner_ref, target_ref, mask_ref, sizes_ref, irreps_ref, amp_ref, first_sem,
    panels_v, amp_v, part, yr, pf, pb, smat, sown, tmat, xsend, xrecv, dense,
    zsp, zrp, zsm, zrm, fx, fr, enc, got, mine, xids, cnt, zcnt, xcnt,
    in_sem, own_sem, ys, yr_sem, xs, xr_sem, zps, zpr, zms, zmr, cs, cr,
    is_, ir, jsend, jrecv, ks, kr, ls, lr,
):
    x, z, c, y = place()
    me = y * NC + c
    dev = lax.axis_index("blk") * NY + y
    slots, width, kdim = panels_v.shape
    tiles = kdim // width
    col = [(((y + dy) % NY) * NC + (c + dc) % NC, device(x, z, (c + dc) % NC, (y + dy) % NY)) for dy, dc in COLUMN]
    xpeers = [device((x + d) % NX, z, c, y) for d in range(1, NX)]
    zpeers = [device(x, (z + d) % NZ, c, y) for d in range(1, NZ)]
    up, down = zpeers[0], zpeers[NZ - 2]
    partner = device(x, z, (c + 1) % NC, y)
    barrier = pltpu.get_barrier_semaphore()
    peers = [p for _, p in col] + xpeers + zpeers
    for p in peers:
        pl.semaphore_signal(barrier, inc=1, device_id=p, device_id_type=MESH)

    small = start([
        pltpu.make_async_copy(a, b, first_sem.at[i])
        for i, (a, b) in enumerate((
            (amp_in, amp_ref), (owner_in, owner_ref), (target_in, target_ref),
            (mask_in, mask_ref), (sizes_in, sizes_ref), (irreps_in, irreps_ref),
        ))
    ])
    reads = start([
        pltpu.make_async_copy(panels_hbm.at[pl.ds(lo, n)], panels_v.at[pl.ds(lo, n)], in_sem.at[g])
        for g, (lo, n) in enumerate(groups)
    ])
    wait(small)

    sources = [irreps_ref[dev * tiles + j] for j in range(tiles)]

    def target_of(s):
        return owner_ref[s] * OWNED + target_ref[s]

    def live_of(s):
        kind = irreps_ref[target_of(s)]
        return [jnp.where(kind == sources[j], mask_ref[j, s], 0) for j in range(tiles)]

    seg_lane = lax.broadcasted_iota(jnp.int32, (8, KPAD), 1)

    def encode(s, row):
        live = live_of(s)
        value = jnp.where(live[0] + live[1] + live[2] + live[3] > 0, target_of(s) + 1, 0)
        return jnp.where(seg_lane == me * SEG + s, value, row)

    lane = lax.broadcasted_iota(jnp.int32, (1, kdim), 1)

    def by_tile(vals):
        v = vals[tiles - 1]
        for j in range(tiles - 2, -1, -1):
            v = jnp.where(lane < (j + 1) * width, vals[j], v)
        return v

    ends = by_tile([sizes_ref[dev * tiles + j] + j * width for j in range(tiles)])
    amp_v[...] = amp_ref[...] * (lane < ends).astype(jnp.bfloat16)

    def one(s, carry):
        mask = by_tile(live_of(s)).astype(jnp.bfloat16)
        acc = lax.dot_general(
            amp_v[...], panels_v[s] * mask, (((1,), (1,)), ((), ())), preferred_element_type=jnp.float32
        )
        low = acc[:, :LANES].reshape(8, 2 * R, LANES)
        high = acc[:, LANES:].reshape(8, 2 * R, width - LANES)
        part[0, :, s] = low[:, :R].astype(jnp.bfloat16)
        part[1, :, s] = low[:, R:].astype(jnp.bfloat16)
        part[2, :, s] = jnp.concatenate([high[:, :R], high[:, R:]], axis=-1).astype(jnp.bfloat16)
        return carry

    halves = ((0, (slots + 1) // 2), ((slots + 1) // 2, slots // 2))

    def y_start(q, k):
        lo, n = groups[k] if q == 0 else halves[k]
        ycp[q, k] = start([
            remote(part.at[q, b, pl.ds(lo, n)], yr.at[q, me, pl.ds(lo, n)], ys.at[q, k, i], yr_sem.at[q, k, i], p)
            for i, (b, p) in enumerate(col)
        ])

    ycp = {}
    for g, (lo, n) in enumerate(groups):
        reads[g].wait()
        lax.fori_loop(lo, lo + n, one, 0)
        if g == 0:
            pl.semaphore_wait(barrier, len(peers))
        y_start(0, g)
        if g == 1:
            enc[...] = lax.fori_loop(0, slots, encode, jnp.zeros((8, KPAD), jnp.int32))
            icp = start([remote(enc, got.at[me], is_.at[i], ir.at[i], p) for i, (b, p) in enumerate(col)])
            got[me] = enc[...]
    y_start(1, 0)
    own = start([pltpu.make_async_copy(part.at[q, me], yr.at[q, me], own_sem.at[q]) for q in range(CHUNKS)])

    wait(icp)
    row = got[0]
    for b in range(1, 8):
        row = row + got[b]
    mine[...] = row
    jcp = start([remote(mine, xids.at[i], jsend.at[i], jrecv.at[i], p) for i, p in enumerate(xpeers)])
    spot = lax.broadcasted_iota(jnp.int32, (SPOTS, KPAD), 0)
    lower = (
        lax.broadcasted_iota(jnp.int32, (SPOTS, SPOTS), 0) >= lax.broadcasted_iota(jnp.int32, (SPOTS, SPOTS), 1)
    ).astype(jnp.bfloat16)

    def ranks(ids, group):
        hit = ids - (group * SPOTS + 1) == spot
        named = jnp.max(hit.astype(jnp.float32), axis=1, keepdims=True)
        wide = jnp.broadcast_to(named, (SPOTS, LANES))
        rank = jnp.dot(lower, wide.astype(jnp.bfloat16), preferred_element_type=jnp.float32)
        return hit, rank * wide

    count = jnp.zeros((1, LANES), jnp.float32)
    for i in range(NX - 1):
        hit, rank = ranks(mine[0:1, :], (x + i + 1) % NX)
        slot = jnp.sum(jnp.where(hit, rank[:, 0:1], 0.0), axis=0, keepdims=True)
        nth = (lax.broadcasted_iota(jnp.int32, (cell, KPAD), 0) + 1).astype(jnp.float32)
        smat[pl.ds(i * cell, cell), :] = (slot == nth).astype(jnp.bfloat16)
        count = jnp.maximum(count, jnp.max(rank, axis=0, keepdims=True))
    sown[...] = (mine[0:1, :] - (x * SPOTS + 1) == spot).astype(jnp.bfloat16)
    cnt[...] = jnp.broadcast_to(count, (8, LANES))
    kcp = start([remote(cnt, zcnt.at[z], ks.at[i], kr.at[i], p) for i, p in enumerate(zpeers)])
    zcnt[z] = cnt[...]
    pf[...] = jnp.zeros(pf.shape, jnp.float32)

    def merge(q):
        def widen(b, carry):
            v = yr[q, b].astype(jnp.float32)
            pf[pl.ds(b * (SEG * R), slots * R), :] = v.reshape(slots * R, LANES)
            return carry

        lax.fori_loop(0, 8, widen, 0)

    def x_start(u):
        q, lo, n = UNITS[u]

        def rows(i, carry):
            r = 2 * i
            a = pf[pl.ds(r, KPAD, stride=R), :].astype(jnp.bfloat16)
            b = pf[pl.ds(r + 1, KPAD, stride=R), :].astype(jnp.bfloat16)
            p = jnp.concatenate([a, b], axis=1)
            pb[i] = p
            m = jnp.dot(smat[...], p, preferred_element_type=jnp.float32).astype(jnp.bfloat16)
            xsend[q, r] = m[:, :LANES]
            xsend[q, r + 1] = m[:, LANES:]
            return carry

        lax.fori_loop(lo // 2, (lo + n) // 2, rows, 0)
        out = []
        for i, p in enumerate(xpeers):
            at = (q, pl.ds(lo, n), pl.ds(i * cell, cell))
            out.append(remote(xsend.at[at], xrecv.at[at], xs.at[u, i], xr_sem.at[u, i], p))
        xcp[u] = start(out)

        def own_rows(i, carry):
            r = 2 * i
            d = jnp.dot(sown[...], pb[i], preferred_element_type=jnp.float32).reshape(NZ, ZT, 2 * LANES)
            dense[q, :, r] = d[:, :, :LANES]
            dense[q, :, r + 1] = d[:, :, LANES:]
            return carry

        lax.fori_loop(lo // 2, (lo + n) // 2, own_rows, 0)

    def gather(u):
        q, lo, n = UNITS[u]

        def rows(i, carry):
            r = 2 * i
            p = jnp.concatenate([xrecv[q, r], xrecv[q, r + 1]], axis=1)
            d = jnp.zeros((SPOTS, 2 * LANES), jnp.float32)
            for k in range(NX - 1):
                d += jnp.dot(tmat[k], p[k * cell : (k + 1) * cell], preferred_element_type=jnp.float32)
            d = d.reshape(NZ, ZT, 2 * LANES)
            dense[q, :, r] += d[:, :, :LANES]
            dense[q, :, r + 1] += d[:, :, LANES:]
            return carry

        lax.fori_loop(lo // 2, (lo + n) // 2, rows, 0)

    def z_step(u, t):
        q, lo, n = UNITS[u]
        mid, hi = lo + n // 2, lo + n
        all_rows, first, second = slice(lo, hi), slice(lo, mid), slice(mid, hi)
        ways = (
            (zsp, zrp, zps, zpr, up, (z + 4 - t) % NZ, first, second),
            (zsm, zrm, zms, zmr, down, (z + 4 + t) % NZ, second, first),
        )
        out = []
        for w, (zs, zr, ss, rs, peer, d, near, rest) in enumerate(ways):
            if t > 0:
                zcp[u][w].wait()
            if t == 0:
                zs[q, 0, near] = dense[q, d, near].astype(jnp.bfloat16)
                at = (q, 0, pl.ds(near.start, n // 2))
            else:
                at = (q, t, pl.ds(lo, n))
                if t == 1:
                    zs[q, 1, near] = (dense[q, d, near] + zr[q, 0, near].astype(jnp.float32)).astype(jnp.bfloat16)
                    zs[q, 1, rest] = dense[q, d, rest].astype(jnp.bfloat16)
                else:
                    both = dense[q, d, all_rows] + zr[q, t - 1, all_rows].astype(jnp.float32)
                    zs[q, t, all_rows] = both.astype(jnp.bfloat16)
            out.append(remote(zs.at[at], zr.at[at], ss.at[u, t], rs.at[u, t], peer))
            out[-1].start()
        zcp[u] = out

    def z_last(u):
        q, lo, n = UNITS[u]
        wait(zcp[u])
        at = slice(lo, lo + n)
        f = dense[q, z, at] + zrp[q, 3, at].astype(jnp.float32) + zrm[q, 3, at].astype(jnp.float32)
        fx[q, 0, at] = f[:, :OWNED]
        fx[q, 1, at] = f[:, OWNED:]
        span = pl.ds(lo, n)
        last[u] = remote(fx.at[q, 1 - c, span], fr.at[q, span], cs.at[u], cr.at[u], partner)
        last[u].start()

    xcp, zcp, last = {}, {}, {}

    def take_y(q):
        if q == 0:
            for g in range(len(groups) - 1):
                wait(ycp[0, g])
            y_start(1, 1)
            wait(ycp[0, len(groups) - 1])
        else:
            if q > 1:
                wait(ycp[q, 0])
            wait(ycp[q, 1])
            if q + 1 < CHUNKS:
                y_start(q + 1, 1)
        own[q].wait()
        merge(q)

    def take_x(u):
        wait(xcp[u])
        gather(u)
        z_step(u, 0)

    def zstep(u, t):
        if t < 4:
            z_step(u, t)
        else:
            z_last(u)

    take_y(0)
    for u in range(NU):
        if UNITS[u][0] == 0:
            x_start(u)
    wait(jcp)
    nth = (lax.broadcasted_iota(jnp.int32, (SPOTS, cell), 1) + 1).astype(jnp.float32)
    for i in range(NX - 1):
        _, rank = ranks(xids[i, 0:1, :], x)
        tmat[i] = (rank[:, 0:1] == nth).astype(jnp.bfloat16)
    wait(kcp)
    cnt[...] = jnp.max(zcnt[...], axis=0)
    lcp = start([remote(cnt, xcnt.at[x], ls.at[i], lr.at[i], p) for i, p in enumerate(xpeers)])
    xcnt[x] = cnt[...]
    for step in PLAN:
        kind, at = step[0], [int(v) for v in step[1:]]
        if kind == "s":
            wait(ycp[1, 0])
            y_start(2, 0)
        elif kind == "y":
            take_y(at[0])
        elif kind == "m":
            x_start(at[0])
        elif kind == "x":
            take_x(at[0])
        else:
            zstep(*at)
    wait(lcp)
    most_ref[...] = jnp.max(xcnt[...], axis=0)
    wait([last[u] for u in range(NU)])
    for q in range(CHUNKS):
        out_ref[q, c] = fx[q, c]
        out_ref[q, 1 - c] = fr[q]


def ladder(cell, ident, owner, target, mask, sizes, irreps, amplitudes, panels):
    slots = panels.shape[0]
    groups, lo = [], 0
    while lo < slots:
        n = min(13 if groups else 5, slots - lo)
        groups.append((lo, n))
        lo += n
    ng = len(groups)
    vmem = pl.BlockSpec(memory_space=pltpu.VMEM)
    dma = pltpu.SemaphoreType.DMA
    bf, f32, i32 = jnp.bfloat16, jnp.float32, jnp.int32
    zbuf = pltpu.VMEM((CHUNKS, 4, R, ZT, LANES), bf)
    return pl.pallas_call(
        functools.partial(ladder_kernel, cell, tuple(groups)),
        out_shape=(
            jax.ShapeDtypeStruct((CHUNKS, NC, R, OWNED, LANES), f32),
            jax.ShapeDtypeStruct((8, LANES), f32),
        ),
        in_specs=[pl.BlockSpec(memory_space=pl.ANY)] * 7,
        out_specs=(vmem, vmem),
        scratch_shapes=[
            pltpu.SMEM(owner.shape, i32),
            pltpu.SMEM(target.shape, i32),
            pltpu.SMEM(mask.shape, i32),
            pltpu.SMEM(sizes.shape, i32),
            pltpu.SMEM(irreps.shape, i32),
            pltpu.VMEM(amplitudes.shape, bf),
            dma((6,)),
            pltpu.VMEM(panels.shape, bf),
            pltpu.VMEM(amplitudes.shape, bf),
            pltpu.VMEM((CHUNKS, 8, slots, R, LANES), bf),
            pltpu.VMEM((CHUNKS, 8, slots, R, LANES), bf),
            pltpu.VMEM((KPAD * R, LANES), f32),
            pltpu.VMEM((R // 2, KPAD, 2 * LANES), bf),
            pltpu.VMEM((3 * cell, KPAD), bf),
            pltpu.VMEM((SPOTS, KPAD), bf),
            pltpu.VMEM((NX - 1, SPOTS, cell), bf),
            pltpu.VMEM((CHUNKS, R, 3 * cell, LANES), bf),
            pltpu.VMEM((CHUNKS, R, 3 * cell, LANES), bf),
            pltpu.VMEM((CHUNKS, NZ, R, ZT, LANES), f32),
            zbuf, zbuf, zbuf, zbuf,
            pltpu.VMEM((CHUNKS, NC, R, OWNED, LANES), f32),
            pltpu.VMEM((CHUNKS, R, OWNED, LANES), f32),
            pltpu.VMEM((8, KPAD), i32),
            pltpu.VMEM((8, 8, KPAD), i32),
            pltpu.VMEM((8, KPAD), i32),
            pltpu.VMEM((NX - 1, 8, KPAD), i32),
            pltpu.VMEM((8, LANES), f32),
            pltpu.VMEM((NZ, 8, LANES), f32),
            pltpu.VMEM((NX, 8, LANES), f32),
            dma((ng,)), dma((CHUNKS,)),
            dma((CHUNKS, ng, 7)), dma((CHUNKS, ng, 7)),
            dma((NU, 3)), dma((NU, 3)),
            dma((NU, 4)), dma((NU, 4)),
            dma((NU, 4)), dma((NU, 4)),
            dma((NU,)), dma((NU,)),
            dma((7,)), dma((7,)),
            dma((3,)), dma((3,)),
            dma((7,)), dma((7,)),
            dma((3,)), dma((3,)),
        ],
        compiler_params=pltpu.CompilerParams(
            collective_id=ident, has_side_effects=True, vmem_limit_bytes=62 * 1024 * 1024
        ),
    )(owner, target, mask, sizes, irreps, amplitudes, panels)


def finish_kernel(sizes_ref, g_ref, occ_ref, vir_ref, out_ref):
    rows, cols_all = out_ref.shape
    first = lax.axis_index("blk") * OWNED
    wide = 2 * cols_all // OWNED
    lane = lax.broadcasted_iota(jnp.int32, (1, wide), 1)
    square = lax.broadcasted_iota(jnp.int32, (rows, rows), 0) == lax.broadcasted_iota(jnp.int32, (rows, rows), 1)
    occ = jnp.sum(jnp.where(square, occ_ref[...], 0.0), axis=1, keepdims=True)

    def tile(t):
        blocks = []
        for c in range(NC):
            piece = [g_ref[pl.ds((q * NC + c) * R * OWNED + t, R, stride=OWNED), :] for q in range(CHUNKS)]
            low = jnp.concatenate(piece[:2], axis=0)
            high = jnp.concatenate([piece[2][:, : LANES // 2], piece[2][:, LANES // 2 :]], axis=0)
            blocks.append(jnp.concatenate([low, high], axis=1))
        return jnp.concatenate(blocks, axis=0)

    for t in range(0, OWNED, 2):
        pair = jnp.concatenate([tile(t), tile(t + 1)], axis=1)
        cols = pl.ds(t * wide // 2, wide)
        ends = jnp.where(lane < wide // 2, sizes_ref[first + t], sizes_ref[first + t + 1] + wide // 2)
        ratio = pair / (occ - vir_ref[:, cols])
        out_ref[:, cols] = jnp.where(lane < ends, ratio, 0.0).astype(jnp.bfloat16)


def finish(sizes, g, occ, vir):
    vmem = pl.BlockSpec(memory_space=pltpu.VMEM)
    return pl.pallas_call(
        finish_kernel,
        out_shape=jax.ShapeDtypeStruct((occ.shape[1], vir.shape[1]), jnp.bfloat16),
        in_specs=[pl.BlockSpec(memory_space=pltpu.SMEM), vmem, vmem, vmem],
        out_specs=vmem,
    )(sizes, g.reshape(CHUNKS * NC * R * OWNED, LANES), occ, vir)


def shards(
    amplitudes,
    panels,
    panel_owner_index,
    panel_target_tile,
    panel_tile_mask,
    tile_sizes,
    tile_irreps,
    occ_energy,
    vir_energy,
):
    args = (panel_owner_index[:, 0], panel_target_tile, panel_tile_mask.T, tile_sizes, tile_irreps, amplitudes, panels)
    summed, most = ladder(CELL, 0, *args)
    summed = lax.cond(
        most[0, 0] <= CELL,
        lambda first, *rest: first,
        lambda first, *rest: ladder(SPOTS, 1, *rest)[0],
        summed, *args,
    )
    return finish(tile_sizes, summed, occ_energy[None, :], vir_energy[None, :])


def solution(mesh):
    return jax.shard_map(
        shards,
        mesh=mesh,
        in_specs=(
            P(None, ("blk", "rep")),
            P(("blk", "rep"), None, None),
            P(("blk", "rep"), None),
            P(("blk", "rep")),
            P(("blk", "rep"), None),
            P(),
            P(),
            P("rep"),
            P("blk"),
        ),
        out_specs=P("rep", "blk"),
        check_vma=False,
    )
```
